128 devices in a mesh: fsdp: 2 (over core), ctx: 16 (over y, x), tp: 4 (over z).
Axes of the slice: x: 4, y: 4, z: 4, core: 2. Of those that a mesh axis runs over, the one named last changes fastest.
Arguments:
- tokens: bfloat16 [2, 2, 1024, 2048], P(None, 'fsdp', 'ctx'), may hold values from -6 to 6
- routes: int32 [2, 2, 1024, 8], P(None, 'fsdp', 'ctx'), may hold values from 0 to 15, all different within a row; in each aligned block of 64 rows (0 to 63, 64 to 127, ..., all dimensions but the last counted through in order) at most 48 rows name the same one
- cotangent: bfloat16 [2, 2, 1024, 2048], P(None, 'fsdp', 'ctx'), may hold values from -6 to 6
- qkv_weight: bfloat16 [3, 2048, 2048], P(None, 'fsdp', 'tp'), may hold values from -0.125 to 0.125
- out_weight: bfloat16 [2048, 2048], P('fsdp', 'tp'), may hold values from -3 to 3
- norm_gains: bfloat16 [2, 2048], P(None, 'fsdp'), may hold values from 0.5 to 1.5
- qk_gains: bfloat16 [2, 128], P(None, 'fsdp'), may hold values from 0.5 to 1.5
- router_weight: bfloat16 [16, 2048], P(None, 'fsdp'), may hold values from -0.0625 to 0.0625
- expert_in: bfloat16 [16, 2, 2048, 1024], P('ctx', None, 'fsdp', 'tp'), may hold values from -0.125 to 0.125
- expert_out: bfloat16 [16, 2048, 1024], P('ctx', 'fsdp', 'tp'), may hold values from -1.5 to 1.5
Outputs:
- layer_out: bfloat16 [2, 2, 1024, 2048], P(None, 'fsdp', 'ctx')
- grad_tokens: float32 [2, 2, 1024, 2048], P(None, 'fsdp', 'ctx')
- grad_qkv: float32 [3, 2048, 2048], P(None, 'fsdp', 'tp')
- grad_out_proj: float32 [2048, 2048], P('fsdp', 'tp')
- grad_norm_gains: float32 [2, 2048], P(None, 'fsdp')
- grad_qk_gains: float32 [2, 128], P(None, 'fsdp')
- grad_router: float32 [16, 2048], P(None, 'fsdp')
- grad_expert_in: float32 [16, 2, 2048, 1024], P('ctx', None, 'fsdp', 'tp')
- grad_expert_out: float32 [16, 2048, 1024], P('ctx', 'fsdp', 'tp')
The draws below stay inside these ranges and needn't reach their ends.
Inputs may be any that keep to these rules, and one draw needn't show every extreme that they name: `routes`: each row names 8 different experts. In every aligned block of 64 positions of a sequence no expert is named by more than 48 rows, a bound that some block reaches.
All inputs are finite; a program needn't handle non-finite values.
Results may differ from the reference program's by a relative error of at most 0.025.
Values may be sent and summed in bfloat16 or wider, within the bound.
A program may use at most 256 MiB of HBM per device.

```python
import math
import jax
import jax.numpy as jnp
import numpy as np
from jax import lax

D = 2048
HEADS = 16
HEAD_DIM = 128
FF = 1024
EXPERTS = 16
TOP = 8
LENGTH = 1024
MICRO = 2
BATCH = 2
GROUP = 64
CAP = 48


def levels(rng, dims, pieces, low, high):
    factor_of = 1.0
    for dim, parts in pieces:
        steps = jax.random.uniform(jax.random.fold_in(jax.random.fold_in(rng, 6), dim), (parts,), jnp.float32, low / len(pieces), high / len(pieces))
        factor_of = factor_of * jnp.repeat(jnp.exp(steps), dims[dim] // parts).reshape((-1,) + (1,) * (len(dims) - 1 - dim))
    return factor_of


def deal_out(rng, own, number, rows, count, top, bound, slope):
    ranking = jax.random.permutation(rng, count)
    packed, usual = shares(count, rows * top, bound, slope, True), shares(count, rows * top, bound, slope, False)
    places = jnp.arange(count)

    def named(lengths, turn):
        used = int((lengths > 0).sum())
        fixed = max(1, used // 4)
        moved = fixed + (places - fixed + turn * (used - fixed)) % max(1, count - fixed)
        return jnp.zeros((count,), jnp.int32).at[ranking[jnp.where(places < fixed, places, moved)]].set(jnp.asarray(lengths, jnp.int32))

    lengths = jnp.where(number % 4 == 0, named(packed, number // 4), named(usual, number - number // 4 - 1))
    mixed = jax.random.permutation(jax.random.fold_in(own, 3), count)
    giver, receiver = mixed[0:count // 2 * 2:2], mixed[1:count // 2 * 2:2]
    room = jnp.minimum(lengths[giver] - 1, bound - lengths[receiver]) // 2
    room = jnp.where((giver == ranking[0]) | (receiver == ranking[0]) | (lengths[receiver] == 0), 0, jnp.maximum(room, 0))
    moved = jax.random.randint(jax.random.fold_in(own, 4), (count // 2,), 0, 1 << 20) % (room + 1)
    lengths = lengths.at[giver].add(-moved).at[receiver].add(moved)
    labels = jnp.searchsorted(jnp.cumsum(lengths), jnp.arange(rows * top), side="right").astype(jnp.int32)
    listing = labels.reshape(top, rows).T
    listing = listing[jax.random.permutation(jax.random.fold_in(own, 1), rows)]
    turn = jax.random.randint(jax.random.fold_in(own, 2), (rows, 1), 0, top)
    return jnp.take_along_axis(listing, (jnp.arange(top)[None, :] + turn) % top, axis=1)


def shares(number_of, total, most, slope, full):
    loads = [(1 << 20) // math.isqrt(grade ** slope) + 1 for grade in range(1, number_of + 1)]
    largest = most if full else min(most, max(-(-total // number_of), total * loads[0] // sum(loads)))
    least = 1 if total - largest >= number_of - 1 else 0
    counts, rest = [largest] + [least] * (number_of - 1), total - largest - least * (number_of - 1)
    while rest > 0:
        movable = [i for i in range(1, number_of) if counts[i] < largest] or [i for i in range(1, number_of) if counts[i] < most]
        whole, budget = sum([loads[i] for i in movable]), rest
        for i in movable:
            extra = min(most - counts[i], max(1, budget * loads[i] // whole), rest)
            counts[i] = counts[i] + extra
            rest = rest - extra
    return np.array(counts)


def centred(own_key, shape, deviation, limit, split=(), held_as=jnp.bfloat16):
    drawn = jax.random.normal(own_key, shape, jnp.float32) * deviation
    if len(split) > 0:
        drawn = levels(own_key, shape, split, -0.22, 0.18) * drawn
    return jnp.clip(drawn, min=-limit, max=limit).astype(held_as)


def setup_inputs(seed: int = 0) -> dict:
    key_list = jax.random.split(jax.random.key(seed), 11)
    tokens = centred(key_list[0], (MICRO, BATCH, LENGTH, D), 1.0, 6.0, ((1, 2), (2, 16)))
    routes_keys = jax.random.split(jax.random.fold_in(key_list[1], 1), MICRO * BATCH * LENGTH // GROUP)
    routes_turns = jax.random.permutation(jax.random.fold_in(key_list[1], 3), MICRO * BATCH * LENGTH // GROUP)
    routes = jax.vmap(lambda own, number: deal_out(jax.random.fold_in(key_list[1], 2), own, number, GROUP, EXPERTS, TOP, CAP, 1))(routes_keys, routes_turns).reshape((MICRO, BATCH, LENGTH, TOP))
    cotangent = centred(key_list[2], (MICRO, BATCH, LENGTH, D), 1.0, 6.0, ((1, 2), (2, 16)))
    qkv_weight = centred(key_list[3], (3, D, HEADS * HEAD_DIM), D ** -0.5, 0.125, ((1, 2), (2, 4)))
    out_weight = centred(key_list[4], (D, HEADS * HEAD_DIM), (max(1, HEADS * HEAD_DIM // (LENGTH // 2))) ** -0.5, 3.0, ((0, 2), (1, 4)))
    norm_gains = jnp.clip(1.0 + 0.1 * jax.random.normal(key_list[5], (2, D), jnp.float32), 0.5, 1.5).astype(jnp.bfloat16)
    qk_gains = jnp.clip(1.0 + 0.1 * jax.random.normal(key_list[6], (2, HEAD_DIM), jnp.float32), 0.5, 1.5).astype(jnp.bfloat16)
    router_weight = centred(key_list[7], (EXPERTS, D), (4 * D) ** -0.5, 0.0625, ((1, 2),))
    expert_in = centred(key_list[8], (EXPERTS, 2, D, FF), D ** -0.5, 0.125, ((0, 16), (2, 2), (3, 4)))
    expert_out = centred(key_list[9], (EXPERTS, D, FF), (max(1, FF // 64)) ** -0.5, 1.5, ((0, 16), (1, 2), (2, 4)))
    return dict(tokens=tokens, routes=routes, cotangent=cotangent, qkv_weight=qkv_weight, out_weight=out_weight, norm_gains=norm_gains, qk_gains=qk_gains, router_weight=router_weight, expert_in=expert_in, expert_out=expert_out)


EPS = 1e-06
BASE = 10000.0
HIGH = lax.Precision.HIGHEST

@jax.custom_vjp
def low(v):
    return lax.optimization_barrier(v.astype(jnp.bfloat16)).astype(jnp.float32)

@jax.custom_vjp
def low_back(v):
    return v

def low_keep(v):
    return (low(v), None)

def low_pass(kept, grad):
    return (grad,)

def back_keep(v):
    return (v, None)

def back_low(kept, grad):
    return (low(grad),)
low.defvjp(low_keep, low_pass)
low_back.defvjp(back_keep, back_low)

def norm_apply(values, scale_gain):
    return values * lax.rsqrt(lax.optimization_barrier(jnp.mean(values * values, axis=-1, keepdims=True)) + EPS) * scale_gain

def rotate(values, positions):
    half_dim = values.shape[-1] // 2
    frequency = BASE ** (-(jnp.arange(half_dim, dtype=jnp.float32) * 2.0 / values.shape[-1]))
    rotation = positions.astype(jnp.float32)[:, None] * frequency[None, :]
    cosine = jnp.cos(rotation)[:, None, :]
    sine_part = jnp.sin(rotation)[:, None, :]
    first_half = values[..., :half_dim]
    second = values[..., half_dim:]
    return jnp.concatenate([first_half * cosine - second * sine_part, second * cosine + first_half * sine_part], axis=-1)

def head_prep(raw_heads, scale_gain, positions):
    return rotate(norm_apply(raw_heads, scale_gain), positions)

def forward(inputs, route_rows, weight_qkv, weight_out, gain_pair, gain_heads, weight_router, weight_in, weight_down):
    positions = jnp.arange(LENGTH, dtype=jnp.int32)
    normed_one = low(norm_apply(inputs, gain_pair[0]))
    projected = low_back(jnp.einsum('ld,kdh->klh', normed_one, low(weight_qkv), precision=HIGH))
    raw_heads = projected.reshape(3, LENGTH, HEADS, HEAD_DIM)
    queries = low(head_prep(raw_heads[0], gain_heads[0], positions))
    all_keys = low(head_prep(raw_heads[1], gain_heads[1], positions))
    all_values = low(raw_heads[2])
    block_rows = min(512, LENGTH)
    score_scale = 1.0 / math.sqrt(HEAD_DIM)

    def attend(query_block):
        scores = low_back(jnp.einsum('qhd,khd->hqk', query_block, all_keys, precision=HIGH) * score_scale)
        weights = low(jax.nn.softmax(scores, axis=-1))
        return jnp.einsum('hqk,khd->qhd', weights, all_values, precision=HIGH)
    head_mixed = lax.map(jax.checkpoint(attend), queries.reshape(LENGTH // block_rows, block_rows, HEADS, HEAD_DIM))
    head_mixed = low(low_back(head_mixed.reshape(LENGTH, HEADS * HEAD_DIM)))
    attended = low_back(jnp.dot(head_mixed, low(weight_out).T, precision=HIGH))
    hidden_one = inputs + attended
    normed_two = low(norm_apply(hidden_one, gain_pair[1]))
    logits = low_back(jnp.dot(normed_two, low(weight_router).T, precision=HIGH))
    router_probs = jax.nn.softmax(logits, axis=-1)
    chosen = jnp.any(route_rows[:, :, None] == jnp.arange(EXPERTS, dtype=jnp.int32)[None, None, :], axis=1)
    gate_values = jnp.where(chosen, router_probs, 0.0)

    def expert_step(running, expert_piece):
        expert_up, expert_down, gate_col = expert_piece
        gate_up = low_back(jnp.einsum('ld,kdf->klf', normed_two, low(expert_up), precision=HIGH))
        hidden = low(jax.nn.silu(gate_up[0]) * gate_up[1])
        result = low_back(jnp.dot(hidden, low(expert_down).T, precision=HIGH))
        return (running + gate_col[:, None] * result, None)
    mixture = lax.scan(jax.checkpoint(expert_step), jnp.zeros_like(inputs), (weight_in, weight_down, gate_values.T))[0]
    return hidden_one + mixture

def reference(tokens, routes, cotangent, qkv_weight, out_weight, norm_gains, qk_gains, router_weight, expert_in, expert_out):
    params = (qkv_weight.astype(jnp.float32), out_weight.astype(jnp.float32), norm_gains.astype(jnp.float32), qk_gains.astype(jnp.float32), router_weight.astype(jnp.float32), expert_in.astype(jnp.float32), expert_out.astype(jnp.float32))
    seq_inputs = tokens.reshape(-1, LENGTH, D).astype(jnp.float32)
    seq_routes = routes.reshape(-1, LENGTH, TOP)
    seq_cotangent = cotangent.reshape(-1, LENGTH, D).astype(jnp.float32)

    def one_sequence(running, item_triple):
        inputs, route_rows, cot_rows = item_triple

        def whole_layer(layer_in, weight_qkv, weight_out, gain_pair, gain_heads, weight_router, weight_in, weight_down):
            return forward(layer_in, route_rows, weight_qkv, weight_out, gain_pair, gain_heads, weight_router, weight_in, weight_down)
        result, pull_back = jax.vjp(whole_layer, inputs, params[0], params[1], params[2], params[3], params[4], params[5], params[6])
        gradients = pull_back(cot_rows)
        running = tuple((earlier + latest for earlier, latest in zip(running, gradients[1:])))
        return (running, (result.astype(jnp.bfloat16), gradients[0]))
    initial = tuple((jnp.zeros_like(member) for member in params))
    totals, (outputs, input_grads) = lax.scan(one_sequence, initial, (seq_inputs, seq_routes, seq_cotangent))
    return (outputs.reshape(tokens.shape), input_grads.reshape(tokens.shape), totals[0], totals[1], totals[2], totals[3], totals[4], totals[5], totals[6])
```

```python
import math

import jax
import jax.numpy as jnp
import numpy as np
from jax import lax
from jax.experimental import pallas as pl
from jax.experimental.pallas import tpu as pltpu
from jax.sharding import PartitionSpec as P

EPS = 1e-06
BASE = 10000.0
HD = 128
E = 16
F32 = jnp.float32
BF = jnp.bfloat16


def rot(x, cos, sin):
    h = x.shape[-1] // 2
    a, b = x[..., :h], x[..., h:]
    return jnp.concatenate([a * cos - b * sin, b * cos + a * sin], axis=-1)


def rot_back(x, cos, sin):
    h = x.shape[-1] // 2
    a, b = x[..., :h], x[..., h:]
    return jnp.concatenate([a * cos + b * sin, b * cos - a * sin], axis=-1)


def inv_rms(v):
    return lax.rsqrt(jnp.mean(v * v, axis=-1, keepdims=True) + EPS)


def norm_back(v, g, du):
    r = inv_rms(v)
    gdu = g * du
    dv = r * gdu - r * r * r * v * jnp.mean(v * gdu, axis=-1, keepdims=True)
    return dv, du * v * r


def nt(a, b):
    return lax.dot_general(a, b, (((1,), (1,)), ((), ())), preferred_element_type=F32)


def tn(a, b):
    return lax.dot_general(a, b, (((0,), (0,)), ((), ())), preferred_element_type=F32)


def nn(a, b):
    return jnp.dot(a, b, preferred_element_type=F32)


def permute(x):
    w = x.shape[-1]
    return x.reshape(2, 4, 16, w).transpose(1, 0, 2, 3).reshape(128, w)


def unpermute(x):
    w = x.shape[-1]
    return x.reshape(4, 2, 16, w).transpose(1, 0, 2, 3).reshape(2, 64, w)


def to_pairs(x):
    return x.reshape(4, 2, 16, 4, HD).transpose(1, 3, 0, 2, 4).reshape(8, 64, HD)


def from_pairs(x):
    return x.reshape(2, 4, 4, 16, HD).transpose(2, 0, 3, 1, 4).reshape(128, 512)


def rope_tables():
    ctx = lax.axis_index("ctx")
    w = BASE ** (-(jnp.arange(64, dtype=F32) * 2.0 / HD))
    pos = (ctx * 64 + jnp.arange(64)).astype(F32)
    ang = pos[:, None] * w[None, :]
    tab = jnp.concatenate([jnp.cos(ang), jnp.sin(ang)], axis=1)
    tab = jnp.broadcast_to(tab.reshape(4, 1, 16, 128), (4, 2, 16, 128)).reshape(128, 128)
    return tab[:, None, :64], tab[:, None, 64:]


def chosen_mask(routes):
    t = lax.axis_index("tp")
    r = lax.dynamic_index_in_dim(routes.reshape(2, 4, 16, 8), t, 1, keepdims=False).reshape(32, 8)
    return jnp.any(r[:, :, None] == jnp.arange(E)[None, None, :], axis=1)


def quarter(x):
    t = lax.axis_index("tp")
    w = x.shape[-1]
    return lax.dynamic_index_in_dim(x.reshape(2, 4, 16, w), t, 1, keepdims=False).reshape(32, w)


MESH = pl.DeviceIdType.MESH
VM = pl.BlockSpec(memory_space=pltpu.VMEM)
ANY = pl.BlockSpec(memory_space=pl.ANY)
SCALE = 1.0 / math.sqrt(HD)


def place():
    f, c, t = lax.axis_index("fsdp"), lax.axis_index("ctx"), lax.axis_index("tp")
    return f, c, t, c // 4, c % 4


def own_pair():
    f, c, _, _, _ = place()
    return c // 8 == f


def hello():
    f, c, t, _, _ = place()
    bar = pltpu.get_barrier_semaphore()
    for k in range(1, 16):
        pl.semaphore_signal(bar, inc=1, device_id={"ctx": (c + k) % 16}, device_id_type=MESH)
    for k in range(1, 4):
        pl.semaphore_signal(bar, inc=1, device_id={"tp": (t + k) % 4}, device_id_type=MESH)
    for k in range(4):
        pl.semaphore_signal(bar, inc=1, device_id={"fsdp": 1 - f, "tp": (t + k) % 4}, device_id_type=MESH)

    @pl.when(c // 8 != f)
    def _():
        for j in range(8):
            pl.semaphore_signal(bar, inc=1, device_id={"fsdp": c // 8, "ctx": 8 * f + j}, device_id_type=MESH)


def greeted():
    f, c, _, _, _ = place()
    pl.semaphore_wait(pltpu.get_barrier_semaphore(), 22 + 8 * (c // 8 + f - 2 * (c // 8) * f))


class Heads:
    def __init__(self, sems, src, dst):
        f, c, _, _, _ = place()
        self.n = sems.take(8)
        self.sems, self.src, self.dst = sems, src, dst

    def copy(self, j):
        f, c, _, _, _ = place()
        dev = {"fsdp": c // 8, "ctx": 8 * f + j}
        return self.sems.remote(self.src(j), self.dst(), dev, self.n + j, self.n + c % 8)

    def start(self, only=range(8)):
        _, c, _, _, _ = place()
        for j in only:
            @pl.when(jnp.logical_not(jnp.logical_and(own_pair(), c % 8 == j)))
            def _():
                self.copy(j).start()

    def wait_recv(self):
        _, c, _, _, _ = place()
        for j in range(8):
            @pl.when(jnp.logical_not(jnp.logical_and(own_pair(), c % 8 == j)))
            def _():
                self.sems.remote(self.src(j), self.dst(), {"fsdp": 1 - place()[0]}, self.n, self.n + j).wait_recv()

    def wait_send(self):
        _, c, _, _, _ = place()
        for j in range(8):
            @pl.when(jnp.logical_not(jnp.logical_and(own_pair(), c % 8 == j)))
            def _():
                self.copy(j).wait_send()


class Sems:
    def __init__(self, send, recv):
        self.send, self.recv, self.n = send, recv, 0

    def take(self, n=1):
        first = self.n
        self.n += n
        return first

    def remote(self, src, dst, dev, i=None, recv_i=None):
        i = self.take() if i is None else i
        return pltpu.make_async_remote_copy(
            src_ref=src, dst_ref=dst, send_sem=self.send.at[i],
            recv_sem=self.recv.at[i if recv_i is None else recv_i],
            device_id=dev, device_id_type=MESH)

    def local(self, src, dst):
        return pltpu.make_async_copy(src, dst, self.send.at[self.take()])


def ctx_dev(y, x):
    return {"ctx": y * 4 + x}


class Gather2:
    def __init__(self, sems, buf, src, m, cut, order=None, first=0, width=None):
        _, _, _, y, x = place()
        self.sems, self.src = sems, src
        width = buf.shape[-1] if width is None else width
        cols = (pl.ds(first, width), pl.ds(first, cut), pl.ds(first + cut, width - cut))
        pick = lambda h: cols[0 if h is None else h + 1]
        if (m if order is None else order) == 0:
            r1, r2 = x, y
            self.dev1 = lambda i: ctx_dev(y, i)
            self.dev2 = lambda i: ctx_dev(i, x)
            self.slot = lambda i, h=None: buf.at[y, i, m, :, pick(h)]
            self.group = lambda i, h=None: buf.at[i, :, m, :, pick(h)]
        else:
            r1, r2 = y, x
            self.dev1 = lambda i: ctx_dev(i, x)
            self.dev2 = lambda i: ctx_dev(y, i)
            self.slot = lambda i, h=None: buf.at[i, x, m, :, pick(h)]
            self.group = lambda i, h=None: buf.at[:, i, m, :, pick(h)]
        self.n1 = (r1, (r1 + 1) % 4, (r1 + 3) % 4)
        self.n2 = (r2, (r2 + 1) % 4, (r2 + 3) % 4)
        self.keep = sems.local(src, self.slot(r1))
        self.sent = []

    def _go(self, src, dst, dev):
        c = self.sems.remote(src, dst, dev)
        c.start()
        self.sent.append(c)
        return c

    def s1(self):
        r = self.n1[0]
        self.keep.start()
        self.a = [self._go(self.src, self.slot(r), self.dev1((r + k) % 4)) for k in (1, 3, 2)]

    def s3(self):
        r, right, left = self.n2
        self.keep.wait()
        for c in self.a:
            c.wait_recv()
        self.c = [self._go(self.group(r), self.group(r), self.dev2(right)), self._go(self.group(r), self.group(r), self.dev2(left))]

    def s4(self):
        r, right, left = self.n2
        self.c[0].wait_recv()
        d0 = self._go(self.group(left, 0), self.group(left, 0), self.dev2(right))
        self.c[1].wait_recv()
        d1 = self._go(self.group(right, 1), self.group(right, 1), self.dev2(left))
        self.d = [d0, d1]

    def s5(self):
        self.d[0].wait_recv()
        self.d[1].wait_recv()

    def fin(self):
        for c in self.sent:
            c.wait_send()


def both(pair, step):
    for g in pair:
        getattr(g, step)()


class WeightGather:
    def __init__(self, sems, src, full, stride, first):
        f, _, t, _, _ = place()
        self.sems, self.src, self.f, self.t = sems, src, f, t
        rows = pl.ds(pl.multiple_of(f * 1024, 1024), 1024)
        top = pl.ds(pl.multiple_of(f * 1024, 1024), 512)
        low = pl.ds(pl.multiple_of(f * 1024 + 512, 512), 512)
        col = lambda z: pl.ds(pl.multiple_of(z * stride + first, 256), 256)
        self.part = lambda z, h=None: full.at[(rows, top, low)[0 if h is None else h + 1], col(z)]
        self.sent, self.crossed = [], []

    def _go(self, src, dst, dev):
        c = self.sems.remote(src, dst, dev)
        c.start()
        self.sent.append(c)
        return c

    def _cross(self, z, src=None):
        c = self._go(self.part(z) if src is None else src, self.part(z), {"fsdp": 1 - self.f})
        self.crossed.append(c)

    def s1(self):
        t = self.t
        self.keep = self.sems.local(self.src, self.part(t))
        self.keep.start()
        self.a = [self._go(self.src, self.part(t), {"tp": (t + 1) % 4}), self._go(self.src, self.part(t), {"tp": (t + 3) % 4})]

    def cross_own(self):
        self._cross(self.t, self.src)

    def s2(self):
        t = self.t
        right, left = (t + 1) % 4, (t + 3) % 4
        self.a[0].wait_recv()
        b0 = self._go(self.part(left, 0), self.part(left, 0), {"tp": right})
        self.a[1].wait_recv()
        b1 = self._go(self.part(right, 1), self.part(right, 1), {"tp": left})
        self.b = [b0, b1]
        self._cross(left)
        self._cross(right)

    def s3(self):
        self.b[0].wait_recv()
        self.b[1].wait_recv()
        self._cross((self.t + 2) % 4)

    def need(self, i):
        if i == 0:
            self.keep.wait()
        self.crossed[i].wait_recv()
        return (self.t + (0, 3, 1, 2)[i]) % 4

    def fin(self):
        for c in self.sent:
            c.wait_send()


def front_kernel(tok_in, router_in, gains_in, qk_in, routes_in, rope, cot, wqkv, wout, ein, eout,
                 wq_o, wo_o, sm_o, xc_o, p_o, oc_o, h1_o, qkv_r_o, of_o, e_o, rt_o, pr_o, y_o, gw_o, yr_o, dxe_o,
                 tok, rtr, gns, qkg_s, routes, wq, wo, tab, tab2, sm, xn1, p, oc, qkv_r, of, es, pr_s, h1_s,
                 qkvs, os, orr, att_s, att_r, msg, xg, cg, win, wdn, dhp, ab_s, g_s, dg_s, xcat, ccat, dab, gh, acc, dxb, yb, gw, dxe,
                 ssem, rsem, *rings):
    f, c, t, y, x = place()
    sems = Sems(ssem, rsem)
    partner = {"fsdp": 1 - f}
    half = pl.ds(pl.multiple_of(f * 1024, 1024), 1024)
    hello()
    first = [sems.local(gains_in, gns), sems.local(tok_in, tok), sems.local(router_in, rtr), sems.local(qk_in, qkg_s), sems.local(routes_in, routes),
             sems.local(rope.at[pl.ds(pl.multiple_of(c * 64, 64), 64)], tab)]
    own = []
    for k in (1, 2, 0):
        own.append(sems.local(wqkv.at[k], wq.at[half, pl.ds(512 * k, 512)]))
    own.append(sems.local(wout, wo.at[half]))
    for cp in first + own:
        cp.start()
    first[0].wait()
    first[1].wait()
    g_own = gns[0:1, :].astype(F32)
    r1 = []
    for z in range(4):
        for m in range(2):
            r1.append(inv_rms(tok[m, 16 * z:16 * z + 16, :].astype(F32)))
            v = tok[m, 16 * z:16 * z + 16, half].astype(F32)
            xn1[32 * z + 16 * m:32 * z + 16 * m + 16, half] = (v * r1[-1] * g_own).astype(BF)
    first[2].wait()
    first[3].wait()
    own_small = jnp.concatenate([rtr[...].astype(F32), gns[...].astype(F32), jnp.zeros((14, 1024), F32)], axis=0)
    sm[f] = own_small
    sm[f, 18:20, 0:64] = qkg_s[...].astype(F32)
    greeted()
    swap_small = sems.remote(sm.at[f], sm.at[f], partner)
    swap_small.start()
    weights = [WeightGather(sems, eout, wdn, 256, 0), WeightGather(sems, ein.at[0], win, 512, 0), WeightGather(sems, ein.at[1], win, 512, 256)]
    for w in weights[:2]:
        w.s1()
    swaps = []
    for k in (1, 2, 0):
        swaps.append(sems.remote(wqkv.at[k], wq.at[half, pl.ds(512 * k, 512)], partner))
    swaps.append(sems.remote(wout, wo.at[half], partner))
    for cp in swaps:
        cp.start()
    for w in weights[:2]:
        w.cross_own()
    rows16 = pl.ds(pl.multiple_of(t * 16, 16), 16)
    cots = [Gather2(sems, cg, cot.at[m, rows16], m, 1024) for m in range(2)]
    both(cots, "s1")

    lhs_own = xn1[:, half]
    for n, k in enumerate((1, 2, 0)):
        own[n].wait()
        p[k] = jnp.dot(lhs_own, wq[half, 512 * k:512 * k + 512], preferred_element_type=F32)
    for cp in first[4:]:
        cp.wait()
    for z in range(4):
        for m in range(2):
            tab2[32 * z + 16 * m:32 * z + 16 * m + 16, :] = tab[16 * z:16 * z + 16, :]
    swap_small.wait_recv()
    rest = pl.ds(pl.multiple_of((1 - f) * 1024, 1024), 1024)
    g_rest = sm[1 - f, 16:17, :]
    for z in range(4):
        for m in range(2):
            v = tok[m, 16 * z:16 * z + 16, rest].astype(F32)
            xn1[32 * z + 16 * m:32 * z + 16 * m + 16, rest] = (v * r1[2 * z + m] * g_rest).astype(BF)
    swap_x = sems.remote(xn1.at[:, rest], xc_o.at[1], partner)
    swap_x.start()
    g2 = jnp.concatenate([sm[0, 17:18, :], sm[1, 17:18, :]], axis=1)
    qkg = jnp.concatenate([sm[0, 18:20, 0:64], sm[1, 18:20, 0:64]], axis=1)
    cos, sin = tab2[:, :128], tab2[:, 128:]
    lhs_rest = xn1[:, rest]
    for n, k in enumerate((1, 2, 0)):
        swaps[n].wait_recv()
        pk = p[k] + jnp.dot(lhs_rest, wq[rest, 512 * k:512 * k + 512], preferred_element_type=F32)
        if k < 2:
            p[k] = pk
        for hl in range(4):
            u = pk[:, 128 * hl:128 * hl + 128]
            if k < 2:
                u = u * inv_rms(u) * qkg[k:k + 1]
                u = u * cos + pltpu.roll(u, 64, 1) * sin
            u = u.astype(BF)
            for m in range(2):
                for z in range(4):
                    qkvs[4 * m + hl, k, 16 * z:16 * z + 16, :] = u[32 * z + 16 * m:32 * z + 16 * m + 16, :]

    heads = Heads(sems, lambda j: qkvs.at[j], lambda: qkv_r.at[:, c])
    heads.start()

    @pl.when(own_pair())
    def _():
        qkv_r[:, c] = qkvs[c % 8]

    weights[0].s2()
    heads.wait_recv()
    mine8 = pl.ds(pl.multiple_of(8 * f, 8), 8)
    rest8 = pl.ds(pl.multiple_of(8 * (1 - f), 8), 8)
    swap_kv = sems.remote(qkv_r.at[pl.ds(1, 2), mine8], qkv_r.at[pl.ds(1, 2), mine8], partner)
    swap_kv.start()
    sums = []
    for part in range(2):
        at = (mine8, rest8)[part]
        if part == 1:
            swap_kv.wait_recv()
        keys = qkv_r[1, at].reshape(512, HD)
        vals = qkv_r[2, at].reshape(512, HD)
        for b in range(4):
            qb = qkv_r[0, pl.ds(8 * f + 2 * b, 2)].reshape(128, HD)
            e = jnp.exp(nt(qb, keys) * SCALE)
            total = jnp.sum(e, axis=1, keepdims=True)
            eb = e.astype(BF)
            ob = jnp.dot(eb, vals, preferred_element_type=F32)
            rows = slice(128 * b, 128 * b + 128)
            es[1 - part, rows, :] = eb
            if part == 0:
                sums.append(total)
                of[rows, :] = ob
            else:
                ri = 1.0 / (sums[b] + total)
                g_s[rows, :] = jnp.broadcast_to(ri, (128, 128))
                ob = (of[rows, :] + ob) * ri
                of[rows, :] = ob
                os[2 * b:2 * b + 2] = ob.astype(BF).reshape(2, 64, HD)
    o_back = Heads(sems, lambda j: os.at[j], lambda: orr.at[c % 8])
    o_back.start()
    both(cots, "s3")
    keep = [sems.local(wq, wq_o), sems.local(sm, sm_o), sems.local(xn1.at[:, half], xc_o.at[0]), sems.local(p.at[pl.ds(0, 2)], p_o), sems.local(qkv_r, qkv_r_o),
            sems.local(of, of_o), sems.local(es, e_o), sems.local(g_s, rt_o)]
    for cp in keep:
        cp.start()

    @pl.when(own_pair())
    def _():
        orr[c % 8] = os[c % 8]

    o_back.wait_recv()
    for j in range(8):
        m, hl = j // 4, j % 4
        for z in range(4):
            oc[0, 32 * z + 16 * m:32 * z + 16 * m + 16, 128 * hl:128 * hl + 128] = orr[j, 16 * z:16 * z + 16, :]

    own[3].wait()
    swaps[3].wait_recv()
    for n in range(4):
        part = nt(oc[0], wo[512 * n:512 * n + 512, :]).astype(BF)
        att_s[:, :, 512 * n:512 * n + 512] = part.reshape(4, 32, 512)
    a0 = sems.take(3)
    att_out = [sems.remote(att_s.at[(t + k) % 4], att_r.at[k - 1], {"tp": (t + k) % 4}, a0 + k - 1) for k in (1, 3, 2)]
    for cp in att_out:
        cp.start()
    weights[1].s2()
    swap_o = sems.remote(oc.at[0], oc.at[1], partner)
    swap_o.start()
    more = [sems.local(wo, wo_o)]
    more[0].start()
    both(cots, "s4")
    xq = jnp.concatenate([tok[m, rows16, :] for m in range(2)], axis=0).astype(F32)
    h1 = xq + att_s[t].astype(F32)
    for cp in att_out:
        cp.wait_recv()
    for k in range(3):
        h1 = h1 + att_r[k].astype(F32)
    weights[2].s1()
    weights[2].cross_own()
    h1_s[...] = h1
    xn2 = (h1 * inv_rms(h1) * g2).astype(BF)
    router = jnp.concatenate([sm[0, :16, :], sm[1, :16, :]], axis=1).astype(BF)
    logits = nt(xn2, router)
    e = jnp.exp(logits - jnp.max(logits, axis=1, keepdims=True))
    pr = e / jnp.sum(e, axis=1, keepdims=True)
    chosen = chosen_in(routes)
    gate = pr * chosen
    pr_s[0] = pr
    pr_s[1] = chosen
    ghi = gate.astype(BF)
    glo = (gate - ghi.astype(F32)).astype(BF)
    tail = jnp.concatenate([ghi, glo, jnp.zeros((32, 96), BF)], axis=1)
    for m in range(2):
        msg[m, :, :2048] = xn2[16 * m:16 * m + 16, :]
        msg[m, :, 2048:] = tail[16 * m:16 * m + 16, :]
    halves = ((0, 1024), (1024, 1152))
    gathers = [[Gather2(sems, xg, msg.at[m, :, pl.ds(first, width)], m, 512, h, first, width) for h, (first, width) in enumerate(halves)] for m in range(2)]
    both(gathers[0], "s1")
    both(gathers[1], "s1")
    more += [sems.local(h1_s, h1_o), sems.local(pr_s, pr_o)]
    for cp in more[-2:]:
        cp.start()
    both(cots, "s5")
    far = pl.ds(pl.multiple_of((1 - f) * 1024, 1024), 1024)
    pass_on = [sems.local(cg.at[:, :, :, :, half], ccat.at[0]), sems.remote(cg.at[:, :, :, :, far], ccat.at[1], partner)]
    for cp in pass_on:
        cp.start()
    swap_o.wait_recv()
    swap_x.wait_recv()
    more.append(sems.local(oc, oc_o))
    more[-1].start()
    both(gathers[0], "s3")
    weights[0].s3()
    both(gathers[1], "s3")

    for n in range(4):
        cols = pl.ds(pl.multiple_of(weights[0].need(n) * 256, 256), 256)
        v = jnp.dot(cg[...].reshape(512, 2048), wdn[:, cols], preferred_element_type=F32).reshape(4, 4, 2, 16, 256)
        for m in range(2):
            dhp[m, :, cols] = v[:, :, m].reshape(256, 256)
        if n == 1:
            both(gathers[0], "s4")
    weights[1].s3()
    both(gathers[1], "s4")
    both(gathers[0], "s5")

    lane = lax.broadcasted_iota(jnp.int32, (256, 128), 1)
    mine = jnp.logical_or(lane == c, lane == c + 16)
    keep[-1].wait()

    def open_gates(m):
        gates = xg[:, :, m, :, 2048:].reshape(256, 128).astype(F32)
        g_s[pl.ds(256 * m, 256), :] = jnp.broadcast_to(jnp.sum(jnp.where(mine, gates, 0.0), axis=1, keepdims=True), (256, 128))
        dg_s[pl.ds(256 * m, 256), :] = jnp.zeros((256, 128), F32)

    def hidden(n, m, z):
        cols = pl.ds(pl.multiple_of(z * 256, 256), 256)
        up = pl.multiple_of(z * 512, 512)
        ab_s[m] = jnp.dot(xg[:, :, m, :, :2048].reshape(256, 2048), win[:, pl.ds(up, 512)], preferred_element_type=F32)
        for i in range(4):
            rows = slice(64 * i, 64 * i + 64)
            both_rows = slice(256 * m + 64 * i, 256 * m + 64 * i + 64)
            a, b, dh, g = ab_s[m, rows, 0:256], ab_s[m, rows, 256:512], dhp[m, rows, cols], g_s[both_rows, 0:1]
            sg = jax.nn.sigmoid(a)
            act = a * sg
            hid = (act * b).astype(BF).astype(F32)
            prod = hid * dh
            dg_s[both_rows, :] = dg_s[both_rows, :] + prod[:, :128] + prod[:, 128:]
            gh[0, m, rows, cols] = (g * hid).astype(BF)
            dhid = g * dh
            dab[0, m, rows, pl.ds(up, 256)] = (dhid * b * sg * (1.0 + a * (1.0 - sg))).astype(BF)
            dab[0, m, rows, pl.ds(pl.multiple_of(up + 256, 256), 256)] = (dhid * act).astype(BF)
        for q in range(4):
            wide = slice(512 * q, 512 * q + 512)
            v = nt(dab[0, m, :, pl.ds(up, 512)], win[wide, pl.ds(up, 512)])
            keep_in = acc.at[m, :, wide] if q < 2 else gw.at[0, pl.ds(256 * m, 256), pl.ds(512 * q - 1024, 512)]
            if n > 0:
                v = v + keep_in[...].astype(F32)
            if n < 3:
                keep_in[...] = v.astype(keep_in.dtype)
            else:
                dxb[:, :, m, :, wide] = v.astype(BF).reshape(4, 4, 16, 512)

    rdx = []

    def send_dx(m):
        dgate = jnp.sum(dg_s[pl.ds(256 * m, 256), :], axis=1, keepdims=True)
        dhi = dgate.astype(BF).astype(F32)
        tail = jnp.where(lane == c, dhi, jnp.where(lane == c + 16, dgate - dhi, 0.0)).astype(BF)
        dxb[:, :, m, :, 2048:] = tail.reshape(4, 4, 16, 128)
        rdx.append([Scatter2(sems, dxb, m, 512, rings[8 * m + 4 * h:8 * m + 4 * h + 4], 16, h, first, width) for h, (first, width) in enumerate(halves)])
        both(rdx[m], "s1")

    def hand_over(z):
        for ref, at in ((dab, pl.ds(pl.multiple_of(z * 512, 512), 512)), (gh, pl.ds(pl.multiple_of(z * 256, 256), 256))):
            pass_on.append(sems.remote(ref.at[0, :, :, at], ref.at[1, :, :, at], partner))
            pass_on[-1].start()

    for n in range(4):
        if n == 3:
            weights[2].s3()
        z = weights[1].need(n)
        weights[2].need(n)
        for m in range(2):
            if n == 0:
                if m == 1:
                    weights[2].s2()
                    both(gathers[1], "s5")
                    pass_on += [sems.local(xg.at[:, :, :, :, half], xcat.at[0]), sems.remote(xg.at[:, :, :, :, far], xcat.at[1], partner)]
                    for cp in pass_on[2:]:
                        cp.start()
                open_gates(m)
            hidden(n, m, z)
            if n == 3:
                send_dx(m)
        hand_over(z)

    def grads(k, n):
        src = ccat if k == 2 else xcat
        rhs = gh[...].reshape(1024, 1024) if k == 2 else dab[:, :, :, 1024 * k:1024 * k + 1024].reshape(1024, 1024)
        at = slice(512 * n, 512 * n + 512)
        gw[k, at, :] = tn(jnp.concatenate([src[o, :, :, m, :, at].reshape(256, 512) for o in range(2) for m in range(2)], axis=0), rhs).astype(BF)

    def keep_grads(k):
        more.append(sems.local(gw.at[k], gw_o.at[k]))
        more[-1].start()

    def half_y(lo):
        for n in range(lo, lo + 2):
            cols = slice(512 * n, 512 * n + 512)
            v = nt(gh[0].reshape(512, 1024), wdn[cols, :]).astype(BF).reshape(2, 4, 4, 16, 512)
            for m in range(2):
                yb[:, :, m, :, cols] = v[m]

    half_y(0)
    both(rdx[0], "s2")
    half_y(2)
    more.append(sems.local(yb, y_o))
    more[-1].start()
    both(rdx[1], "s2")
    for cp in (pass_on[0], pass_on[2]):
        cp.wait()
    for cp in [pass_on[1]] + pass_on[3:]:
        cp.wait_recv()
    grads(0, 0)
    both(rdx[0], "s3")
    grads(0, 1)
    keep_grads(0)
    grads(1, 0)
    both(rdx[1], "s3")
    ry = [Scatter2(sems, yb, m, 1024, (yr_o.at[m, 0], yr_o.at[m, 1], None, None)) for m in range(2)]
    both(ry, "s1")
    grads(1, 1)
    keep_grads(1)
    grads(2, 0)
    grads(2, 1)
    keep_grads(2)
    both(cots, "fin")
    both(gathers[0] + gathers[1], "fin")
    for w in weights:
        w.fin()
    heads.wait_send()
    o_back.wait_send()
    for cp in keep[:-1]:
        cp.wait()
    for cp in swaps + [swap_small, swap_kv, swap_x, swap_o]:
        cp.wait_send()
    for cp in [pass_on[1]] + pass_on[3:]:
        cp.wait_send()
    for cp in att_out:
        cp.wait_send()
    for m in range(2):
        both(rdx[m], "s5")
        for h, (first, width) in enumerate(halves):
            dxe[16 * m:16 * m + 16, first:first + width] = rdx[m][h].result(pl.ds(0, 16))
    more.append(sems.local(dxe, dxe_o))
    more[-1].start()
    both(rdx[0] + rdx[1], "fin")
    for r in ry:
        for cp in r.a:
            cp.wait()
    for cp in more:
        cp.wait()


class GatherZ:
    def __init__(self, sems, buf):
        _, _, t, _, _ = place()
        self.sems, self.buf, self.t = sems, buf, t
        self.right, self.left = (t + 1) % 4, (t + 3) % 4
        self.sent = []

    def _go(self, ref, z):
        c = self.sems.remote(ref, ref, {"tp": z})
        c.start()
        self.sent.append(c)
        return c

    def s1(self):
        own = self.buf.at[self.t]
        self.a = [self._go(own, self.right), self._go(own, self.left)]

    def s2(self):
        self.a[0].wait_recv()
        b0 = self._go(self.buf.at[self.left, :, pl.ds(0, 1024)], self.right)
        self.a[1].wait_recv()
        self.b = [b0, self._go(self.buf.at[self.right, :, pl.ds(1024, 1024)], self.left)]

    def s3(self):
        for c in self.b:
            c.wait_recv()

    def fin(self):
        for c in self.sent:
            c.wait_send()


class SumZ:
    def __init__(self, sems, buf, ra, rb):
        _, _, t, _, _ = place()
        self.sems, self.buf, self.ra, self.rb = sems, buf, ra, rb
        self.n = (t, (t + 1) % 4, (t + 2) % 4, (t + 3) % 4)
        self.sent = []

    def _go(self, src, dst, z):
        c = self.sems.remote(src, dst, {"tp": z})
        c.start()
        self.sent.append(c)
        return c

    def s1(self):
        _, right, opp, left = self.n
        self.a = [self._go(self.buf.at[opp, :, pl.ds(1024 * h, 1024)], self.ra.at[h], z) for h, z in ((0, right), (1, left))]

    def s2(self):
        _, right, opp, left = self.n
        self.b = []
        for h, z in ((0, right), (1, left)):
            self.a[h].wait_recv()
            at = (z, slice(None), pl.ds(1024 * h, 1024))
            self.buf[at] = (self.buf[at].astype(F32) + self.ra[h].astype(F32)).astype(BF)
            self.b.append(self._go(self.buf.at[z], self.rb.at[h], z))

    def result(self):
        for c in self.b:
            c.wait_recv()
        return self.buf[self.n[0]].astype(F32) + self.rb[0].astype(F32) + self.rb[1].astype(F32)

    def fin(self):
        for c in self.sent:
            c.wait_send()


def chosen_in(routes):
    _, _, t, _, _ = place()
    expert = lax.broadcasted_iota(jnp.int32, (E, 64), 0)
    pick = (lax.broadcasted_iota(jnp.int32, (16, 64), 1) == 16 * t + lax.broadcasted_iota(jnp.int32, (16, 64), 0)).astype(F32).astype(BF)
    parts = []
    for m in range(2):
        hit = routes[m, 0:1, :] == expert
        for j in range(1, 8):
            hit = jnp.logical_or(hit, routes[m, j:j + 1, :] == expert)
        parts.append(nt(pick, hit.astype(F32).astype(BF)))
    return jnp.concatenate(parts, axis=0)


def rope_const():
    w = BASE ** (-(np.arange(64, dtype=np.float32) * np.float32(2.0) / np.float32(HD)))
    ang = np.arange(1024, dtype=np.float32)[:, None] * w.astype(np.float32)[None, :]
    cos, sin = np.cos(ang), np.sin(ang)
    return np.concatenate([cos, cos, -sin, sin], axis=1).astype(np.float32)


def front(tok, cot, wqkv, wout, small, ein, eout, routes):
    sd = jax.ShapeDtypeStruct
    v = pltpu.VMEM
    shapes = [
        sd((2048, 1536), BF), sd((2048, 512), BF), sd((2, 32, 1024), F32), sd((2, 128, 1024), BF), sd((2, 128, 512), F32),
        sd((2, 128, 512), BF), sd((32, 2048), F32), sd((3, 16, 64, HD), BF), sd((512, HD), F32),
        sd((2, 512, 512), BF), sd((512, 128), F32), sd((2, 32, 16), F32), sd((4, 4, 2, 16, 2048), BF), sd((3, 1024, 1024), BF), sd((2, 2, 4, 16, 1024), BF), sd((32, 2176), F32)]
    rings = []
    for width in (1024, 1152, 1024, 1152):
        rings += Scatter2.scratch(16, width, 512)
    outs = pl.pallas_call(
        front_kernel,
        out_shape=shapes,
        in_specs=[ANY] * 11,
        out_specs=[ANY] * 16,
        scratch_shapes=[
            v((2, 64, 2048), BF), v((16, 1024), BF), v((2, 1024), BF), v((2, 64), BF), v((2, 8, 64), jnp.int32),
            v((2048, 1536), BF), v((2048, 512), BF), v((64, 256), F32), v((128, 256), F32),
            v((2, 32, 1024), F32), v((128, 2048), BF), v((3, 128, 512), F32), v((2, 128, 512), BF), v((3, 16, 64, HD), BF), v((512, HD), F32),
            v((2, 512, 512), BF), v((2, 32, 16), F32), v((32, 2048), F32),
            v((8, 3, 64, HD), BF), v((8, 64, HD), BF), v((8, 64, HD), BF),
            v((4, 32, 2048), BF), v((3, 32, 2048), BF), v((2, 16, 2176), BF),
            v((4, 4, 2, 16, 2176), BF), v((4, 4, 2, 16, 2048), BF), v((2048, 2048), BF), v((2048, 1024), BF),
            v((2, 256, 1024), F32), v((2, 256, 512), F32), v((512, 128), F32), v((512, 128), F32),
            v((2, 4, 4, 2, 16, 1024), BF), v((2, 4, 4, 2, 16, 1024), BF), v((2, 2, 256, 2048), BF), v((2, 2, 256, 1024), BF), v((2, 256, 1024), F32),
            v((4, 4, 2, 16, 2176), BF), v((4, 4, 2, 16, 2048), BF), v((3, 1024, 1024), BF), v((32, 2176), F32),
            pltpu.SemaphoreType.DMA((192,)), pltpu.SemaphoreType.DMA((192,))] + rings,
        compiler_params=pltpu.CompilerParams(collective_id=0, has_side_effects=True, vmem_limit_bytes=62 << 20),
        name="front",
    )(tok, *small, routes, jnp.asarray(rope_const()), cot, wqkv, wout, ein, eout)
    names = ("wq", "wo", "sm", "xc", "p", "oc", "h1", "qkv_r", "of", "e", "rt", "pr", "y", "gw", "yr", "dxe")
    return dict(zip(names, outs))


def add_rows(n, rows, step, body):
    def outer(i, _):
        def inner(j, _):
            body(i, pl.ds(pl.multiple_of(j * step, step), step))
            return 0
        return lax.fori_loop(0, rows // step, inner, 0)
    lax.fori_loop(0, n, outer, 0)


class Scatter2:
    def __init__(self, sems, buf, m, cut, bufs, step=16, order=None, first=0, width=None):
        _, _, _, y, x = place()
        self.order = m if order is None else order
        self.a = None
        self.sems, self.buf, self.m, self.step = sems, buf, m, step
        self.rows, width = buf.shape[-2], buf.shape[-1] if width is None else width
        self.lo, self.hi, self.all = pl.ds(first, cut), pl.ds(first + cut, width - cut), pl.ds(first, width)
        self.ra_lo, self.ra_hi, self.rb, self.sb = bufs
        if self.order == 0:
            r1, r2 = y, x
            self.dev1, self.dev2 = (lambda i: ctx_dev(i, x)), (lambda i: ctx_dev(y, i))
        else:
            r1, r2 = x, y
            self.dev1, self.dev2 = (lambda i: ctx_dev(y, i)), (lambda i: ctx_dev(i, x))
        ring = lambda r: (r, (r + 1) % 4, (r + 2) % 4, (r + 3) % 4)
        self.n1, self.n2 = ring(r1), ring(r2)
        self.sent = []

    @staticmethod
    def scratch(rows, width, cut):
        return [pltpu.VMEM((4, rows, cut), BF), pltpu.VMEM((4, rows, width - cut), BF), pltpu.VMEM((2, 4, rows, width), BF),
                pltpu.VMEM((3, rows, width), BF)]

    def idx(self, g, s, rows, cols):
        return (g, s, self.m, rows, cols) if self.order == 0 else (s, g, self.m, rows, cols)

    def group(self, g, cols):
        return self.buf.at[self.idx(g, slice(None), slice(None), cols)]

    def slot(self, s, cols):
        return self.buf.at[self.idx(self.n1[0], s, slice(None), cols)]

    def _go(self, src, dst, dev):
        c = self.sems.remote(src, dst, dev)
        c.start()
        self.sent.append(c)
        return c

    def _acc(self, g, s, rows, cols, *terms):
        at = self.idx(g, s, rows, cols)
        total = self.buf[at].astype(F32)
        for v in terms:
            total = total + v.astype(F32)
        return at, total

    def s1(self):
        r, right, opp, left = self.n1
        self.a = [self._go(self.group(opp, self.lo), self.ra_lo, self.dev1(right)), self._go(self.group(opp, self.hi), self.ra_hi, self.dev1(left))]

    def s2(self):
        r, right, opp, left = self.n1
        self.b = []
        for n, (g, cols, ra) in enumerate(((right, self.lo, self.ra_lo), (left, self.hi, self.ra_hi))):
            if self.a:
                self.a[n].wait_recv()

            def body(i, rows):
                at, total = self._acc(g, i, rows, cols, ra[i, rows, :])
                self.buf[at] = total.astype(BF)
            add_rows(4, self.rows, self.step, body)
            self.b.append(self._go(self.group(g, self.all), self.rb.at[n], self.dev1(g)))

    def s3(self):
        for cp in self.b:
            cp.wait_recv()

        def body(i, rows):
            at, total = self._acc(self.n1[0], i, rows, self.all, self.rb[0, i, rows, :], self.rb[1, i, rows, :])
            self.buf[at] = total.astype(BF)
        add_rows(4, self.rows, self.step, body)
        self.c = [self._go(self.slot(self.n2[k], self.all), self.sb.at[k - 1], self.dev2(self.n2[k])) for k in (1, 3, 2)]

    def s5(self):
        for cp in self.c:
            cp.wait_recv()

    def result(self, rows):
        return self._acc(self.n1[0], self.n2[0], rows, self.all, *[self.sb[k, rows, :] for k in range(3)])[1]

    def fin(self):
        for c in self.sent:
            c.wait_send()


class ScatterZ:
    def __init__(self, sems, view, ra, rb):
        _, _, t, _, _ = place()
        self.sems, self.view, self.ra, self.rb = sems, view, ra, rb
        self.n = (t, (t + 1) % 4, (t + 2) % 4, (t + 3) % 4)
        self.sent = []

    @staticmethod
    def scratch(width):
        return [pltpu.VMEM((2, 1024, width // 2), BF), pltpu.VMEM((2, 1024, width), BF)]

    def _go(self, src, dst, z):
        c = self.sems.remote(src, dst, {"tp": z})
        c.start()
        self.sent.append(c)
        return c

    def s1(self):
        r, right, opp, left = self.n
        self.a = [self._go(self.view(opp, h), self.ra.at[h], z) for h, z in ((0, right), (1, left))]

    def s2(self):
        r, right, opp, left = self.n
        self.b = []
        for h, z in ((0, right), (1, left)):
            self.a[h].wait_recv()
            half = self.view(z, h)

            def body(i, rows):
                half[rows, :] = (half[rows, :].astype(F32) + self.ra[h, rows, :].astype(F32)).astype(BF)
            add_rows(1, 1024, 64, body)
            self.b.append(self._go(self.view(z), self.rb.at[h], z))

    def s3(self, put):
        for cp in self.b:
            cp.wait_recv()
        mine = self.view(self.n[0])

        def body(i, rows):
            put(rows, (mine[rows, :].astype(F32) + self.rb[0, rows, :].astype(F32) + self.rb[1, rows, :].astype(F32)).astype(BF))
        add_rows(1, 1024, 64, body)

    def fin(self):
        for c in self.sent:
            c.wait_send()


class SumPlane:
    def __init__(self, sems, src, landing):
        _, _, _, y, x = place()
        self.src, self.landing = src, landing
        n = sems.take(6)
        self.step = [[sems.remote(src.at[a], landing.at[a, k - 1], ctx_dev(y, (x + k) % 4) if a == 0 else ctx_dev((y + k) % 4, x), n + 3 * a + k - 1)
                      for k in (1, 3, 2)] for a in range(2)]

    def start(self, a):
        for cp in self.step[a]:
            cp.start()

    def sum(self, a):
        for cp in self.step[a]:
            cp.wait_recv()
        total = self.src[a].astype(F32)
        for k in range(3):
            total = total + self.landing[a, k].astype(F32)
        return total

    def fin(self):
        for cp in self.step[0] + self.step[1]:
            cp.wait_send()


def back_kernel(dxe_in, tok_in, cot_in, pr_in, sm_in, xc_in, p_in, oc_in, h1_in, qkv_r_in, of_in, e_in, rt_in, rope, y_in, gw_in, yr_in, wq_in, wo_in,
                lay_o, gt_o, gall_o, sg_o, ge_o, g1_o,
                sg, g1f, dxe, lay, gt, ge, tok, cot, prs, sm, xc, p, oc, h1, qkv_r, of, rinv,
                wq, wo, tab, tab2, gw, yb, yr, pm, dA, do_s, do_r, dkv_o, dkv_p, bv_s, bv_r, bqk_s, bqk_r, gall, du, dp, dx1_s, dx1_a, dx1_b,
                dAc, ar, chunk, part, part_s, part_r, part_z, part_zr, part_c, part_cr, g1_s, g1_r, g1_z, ssem, rsem, *rings):
    f, c, t, y, x = place()
    hello()
    sems = Sems(ssem, rsem)
    partner = {"fsdp": 1 - f}
    rows16 = pl.ds(pl.multiple_of(t * 16, 16), 16)
    pairs = [(dxe_in, dxe), (h1_in, h1), (cot_in.at[:, rows16], cot), (pr_in, prs), (sm_in, sm), (y_in, yb), (yr_in, yr), (wo_in, wo), (qkv_r_in, qkv_r), (of_in, of),
             (e_in, pm), (rt_in, rinv), (oc_in, oc), (rope.at[pl.ds(pl.multiple_of(c * 64, 64), 64)], tab), (gw_in, gw), (p_in, p), (xc_in, xc),
             (wq_in, wq), (tok_in.at[:, rows16], tok)]
    load = [sems.local(*pair) for pair in pairs]
    for cp in load:
        cp.start()
    ry = [Scatter2(sems, yb, m, 1024, (yr.at[m, 0], yr.at[m, 1]) + tuple(rings[4 * m + 2:4 * m + 4])) for m in range(2)]
    rar = [[Scatter2(sems, ar.at[k], m, 256, rings[8 * k + 8 + 4 * m:8 * k + 12 + 4 * m], 32) for m in range(2)] for k in range(4)]

    def wide(z, h=None):
        first = (z % 2) * 512 + (0 if h is None else 256 * h)
        return gw.at[z // 2, :, pl.ds(pl.multiple_of(first, 256), 512 if h is None else 256)]

    def narrow(z, h=None):
        first = z * 256 + (0 if h is None else 128 * h)
        return gw.at[2, :, pl.ds(pl.multiple_of(first, 128), 256 if h is None else 128)]

    rz = [ScatterZ(sems, wide, *rings[40:42]), ScatterZ(sems, narrow, *rings[42:44])]
    for cp in load[:5]:
        cp.wait()
    g1 = jnp.concatenate([sm[0, 16:17, :], sm[1, 16:17, :]], axis=1)
    g2 = jnp.concatenate([sm[0, 17:18, :], sm[1, 17:18, :]], axis=1)
    qkg = jnp.concatenate([sm[0, 18:20, 0:64], sm[1, 18:20, 0:64]], axis=1)
    router = jnp.concatenate([sm[0, :16, :], sm[1, :16, :]], axis=1).astype(BF)
    hv = h1[...]
    r2 = inv_rms(hv)
    xn2 = (hv * r2 * g2).astype(BF)
    pr, chosen = prs[0], prs[1]
    cq = cot[...].reshape(32, 2048).astype(F32)
    got = dxe[...]
    dpr = chosen * (got[:, 2048:2064] + got[:, 2064:2080])
    dl = (pr * (dpr - jnp.sum(pr * dpr, axis=1, keepdims=True))).astype(BF)
    du2 = got[:, :2048] + jnp.dot(dl, router, preferred_element_type=F32)
    gdu = g2 * du2
    dh1 = cq + r2 * gdu - r2 * r2 * r2 * hv * jnp.mean(hv * gdu, axis=1, keepdims=True)
    dA[t] = dh1.astype(BF)
    greeted()
    d0 = sems.take(3)
    dA_out = [sems.remote(dA.at[t], dA.at[t], {"tp": (t + k) % 4}, d0 + k - 1) for k in (1, 3, 2)]
    for cp in dA_out:
        cp.start()
    load[5].wait()
    load[6].wait()
    both(ry, "s2")
    load[13].wait()
    for z in range(4):
        for m in range(2):
            tab2[32 * z + 16 * m:32 * z + 16 * m + 16, :] = tab[16 * z:16 * z + 16, :]
    g_router = tn(dl, xn2)
    g_g2 = jnp.sum(du2 * hv * r2, axis=0, keepdims=True)
    for h in range(2):
        cols = slice(1024 * h, 1024 * h + 1024)
        part[h] = jnp.zeros((32, 1024), F32)
        part[h, 0:16, :] = g_router[:, cols]
        part[h, 17:18, :] = g_g2[:, cols]
    load[7].wait()
    for cp in dA_out:
        cp.wait_recv()
    dA2 = dA[...].reshape(128, 2048)
    fo = pl.multiple_of((1 - f) * 1024, 1024)
    fm = pl.multiple_of(f * 1024, 1024)
    swap_a = sems.remote(dA.at[:, :, pl.ds(fo, 1024)], dAc.at[1], partner)
    swap_a.start()
    dd = jnp.dot(dA2, wo[...], preferred_element_type=F32).astype(BF)
    for hl in range(4):
        for m in range(2):
            for z in range(4):
                do_s[4 * m + hl, 16 * z:16 * z + 16, :] = dd[32 * z + 16 * m:32 * z + 16 * m + 16, 128 * hl:128 * hl + 128]
    do_out = Heads(sems, lambda j: do_s.at[j], lambda: do_r.at[c % 8])
    do_out.start()

    @pl.when(own_pair())
    def _():
        do_r[c % 8] = do_s[c % 8]

    both(ry, "s3")

    def grads(lhs, rhs, k):
        for n in range(2):
            v = tn(lhs[:, 512 * n:512 * n + 512], rhs).astype(BF)
            ar[k, 2 * n:2 * n + 2] = v.reshape(2, 4, 2, 32, 512)
        both(rar[k], "s1")

    load[14].wait()
    both(rz, "s1")
    dAc[0] = dA[:, :, pl.ds(fm, 1024)]
    load[12].wait()
    mine8 = pl.ds(pl.multiple_of(8 * f, 8), 8)
    rest8 = pl.ds(pl.multiple_of(8 * (1 - f), 8), 8)
    for cp in load[8:12]:
        cp.wait()
    keys = [qkv_r[1, at].reshape(512, HD) for at in (rest8, mine8)]
    vals = [qkv_r[2, at].reshape(512, HD) for at in (rest8, mine8)]
    queries = qkv_r[0, mine8].reshape(512, HD)
    swap_a.wait_recv()
    grads(dAc[...].reshape(256, 1024), oc[...].reshape(256, 512), 3)
    do_out.wait_recv()

    do_all = do_r[...].reshape(512, HD).astype(F32)
    ri = rinv[:, 0:1]
    scaled = (do_all * ri).astype(BF)
    dkv_o[1] = tn(pm[0], scaled).astype(BF)
    swap_v = sems.remote(dkv_o.at[1], dkv_p.at[1], partner)
    swap_v.start()
    dv = tn(pm[1], scaled)
    delta = ri * jnp.sum(do_all * of[...], axis=1, keepdims=True)
    for hk in range(2):
        dS = (pm[hk].astype(F32) * (nt(scaled, vals[hk]) - delta)).astype(BF)
        dk = tn(dS, queries)
        d = jnp.dot(dS, keys[hk], preferred_element_type=F32)
        dq = d if hk == 0 else dq + d
        if hk == 0:
            dkv_o[0] = (dk * SCALE).astype(BF)
            swap_k = sems.remote(dkv_o.at[0], dkv_p.at[0], partner)
            swap_k.start()
            swap_v.wait_recv()
            bv_s[...] = (dv + dkv_p[1].astype(F32)).astype(BF).reshape(8, 64, HD)
            v_out = Heads(sems, lambda j: bv_s.at[j], lambda: bv_r.at[c % 8])
            v_out.start()

            @pl.when(own_pair())
            def _():
                bv_r[c % 8] = bv_s[c % 8]
            both(rar[3], "s2")
    bqk_s[:, 0] = (dq * SCALE).astype(BF).reshape(8, 64, HD)
    swap_k.wait_recv()
    bqk_s[:, 1] = (dk * SCALE + dkv_p[0].astype(F32)).astype(BF).reshape(8, 64, HD)
    qk_out = Heads(sems, lambda j: bqk_s.at[j], lambda: bqk_r.at[c % 8])
    qk_out.start()

    @pl.when(own_pair())
    def _():
        bqk_r[c % 8] = bqk_s[c % 8]

    for cp in load[15:19]:
        cp.wait()
    v_out.wait_recv()
    for j in range(8):
        m, hl = j // 4, j % 4
        for z in range(4):
            dp[0, 32 * z + 16 * m:32 * z + 16 * m + 16, 1024 + 128 * hl:1024 + 128 * hl + 128] = bv_r[j, 16 * z:16 * z + 16, :]
    swap_d = {}

    def share(k):
        at = pl.ds(512 * k, 512)
        swap_d[k] = sems.remote(dp.at[0, :, at], dp.at[1, :, at], partner)
        swap_d[k].start()

    def qkv_grads(k):
        swap_d[k].wait_recv()
        grads(xc[...].reshape(256, 1024), dp[:, :, 512 * k:512 * k + 512].reshape(256, 512), k)

    gat = {}

    def publish(k):
        both(rar[k], "s5")
        gat[k] = []
        for m in range(2):
            chunk[k, m] = rar[k][m].result(pl.ds(0, 32)).astype(BF)
            gat[k].append(Gather2(sems, gall.at[k], chunk.at[k, m], m, 256))
        both(gat[k], "s1")

    def dxn1_part(n):
        cols = slice(512 * n, 512 * n + 512)
        dx1_s[:, :, cols] = nt(dp[0], wq[cols, :]).astype(BF).reshape(4, 32, 512)

    cos, sin = tab2[:, :128], tab2[:, 128:]

    def head_back(k):
        total = jnp.zeros((1, HD), F32)
        for hl in range(4):
            cols = slice(128 * hl, 128 * hl + 128)
            u = du[k, :, cols]
            u = u * cos - pltpu.roll(u, 64, 1) * sin
            pk = p[k, :, cols]
            r = inv_rms(pk)
            gu = qkg[k:k + 1] * u
            dp[0, :, 512 * k + 128 * hl:512 * k + 128 * hl + 128] = (r * gu - r * r * r * pk * jnp.mean(pk * gu, axis=1, keepdims=True)).astype(BF)
            total = total + jnp.sum(u * pk * r, axis=0, keepdims=True)
        share(k)
        part[0, 18 + k:19 + k, 0:64] = total[:, 0:64]
        part[1, 18 + k:19 + k, 0:64] = total[:, 64:128]

    share(2)
    both(rar[3], "s3")
    qkv_grads(2)
    rz[0].s2()
    qk_out.wait_recv()
    for j in range(8):
        m, hl = j // 4, j % 4
        for z in range(4):
            rows, src = slice(32 * z + 16 * m, 32 * z + 16 * m + 16), slice(16 * z, 16 * z + 16)
            for k in range(2):
                du[k, rows, 128 * hl:128 * hl + 128] = bqk_r[j, k, src, :].astype(F32)
    head_back(0)
    both(rar[2], "s2")
    head_back(1)
    qkv_grads(0)
    qkv_grads(1)
    part_s[...] = part[1 - f].astype(BF)
    swap_p = sems.remote(part_s, part_r, partner)
    swap_p.start()
    publish(3)
    both(rar[2], "s3")
    both(rar[0], "s2")
    dxn1_part(0)
    both(rar[1], "s2")
    dxn1_part(1)
    both(gat[3], "s3")
    publish(2)
    dxn1_part(2)
    both(rar[0], "s3")
    dxn1_part(3)
    dx1 = SumZ(sems, dx1_s, dx1_a, dx1_b)
    dx1.s1()
    both(rar[1], "s3")
    swap_p.wait_recv()
    total = (part[f] + part_r[...].astype(F32)).astype(BF)
    for z in range(4):
        part_z[z] = total[:, 256 * z:256 * z + 256]
    z0 = sems.take(3)
    pz_out = [sems.remote(part_z.at[(t + k) % 4], part_zr.at[k - 1], {"tp": (t + k) % 4}, z0 + k - 1) for k in range(1, 4)]
    for cp in pz_out:
        cp.start()
    both(gat[2], "s3")
    publish(0)
    both(gat[3], "s4")
    publish(1)
    dx1.s2()
    both(ry, "s5")
    mix = jnp.concatenate([ry[m].result(pl.ds(0, 16)) for m in range(2)], axis=0)
    lay[t] = (hv + mix).astype(BF)
    lay_all = GatherZ(sems, lay)
    lay_all.s1()
    both(gat[2], "s4")
    both(gat[0], "s3")
    tot = part_z[t].astype(F32)
    for k in range(3):
        pz_out[k].wait_recv()
        tot = tot + part_zr[k].astype(F32)
    part_c[0] = tot.astype(BF)
    small_sum = SumPlane(sems, part_c, part_cr)
    small_sum.start(0)
    both(gat[1], "s3")
    xv = tok[...].reshape(32, 2048).astype(F32)
    r1 = inv_rms(xv)
    dxn1 = dx1.result()
    gdu = g1 * dxn1
    gtv = dh1 + r1 * gdu - r1 * r1 * r1 * xv * jnp.mean(xv * gdu, axis=1, keepdims=True)
    gt[t] = gtv.astype(BF)
    gt_all = GatherZ(sems, gt)
    gt_all.s1()
    g_g1 = jnp.sum(dxn1 * xv * r1, axis=0, keepdims=True)
    for i in range(16):
        g1_s[0, i // 8, i % 8:i % 8 + 1, :] = g_g1[:, 128 * i:128 * i + 128]
    gain_sum = SumPlane(sems, g1_s, g1_r)
    gain_sum.start(0)
    rz[1].s2()
    both(gat[0], "s4")
    part_c[1] = small_sum.sum(0).astype(BF)
    small_sum.start(1)
    lay_all.s2()
    both(gat[2], "s5")
    both(gat[3], "s5")
    out_all = [sems.local(gall.at[k], gall_o.at[k]) for k in (2, 3)]
    for cp in out_all:
        cp.start()
    both(gat[1], "s4")
    g1_s[1] = gain_sum.sum(0)
    gain_sum.start(1)
    gt_all.s2()
    for cp in dA_out:
        cp.wait_send()
    for h in (do_out, v_out, qk_out):
        h.wait_send()
    for cp in [swap_d[k] for k in range(3)] + [swap_a, swap_p, swap_v, swap_k]:
        cp.wait_send()
    sg[t] = small_sum.sum(1)
    g0 = sems.take(3)
    sg_out = [sems.remote(sg.at[t], sg.at[t], {"tp": (t + k) % 4}, g0 + k - 1) for k in range(1, 4)]
    for cp in sg_out:
        cp.start()
    both(ry, "fin")
    for k in range(4):
        both(rar[k], "fin")
    tot = gain_sum.sum(1)
    g1_s[2] = tot
    b0 = sems.take(8)
    gb_out = []
    for k in range(1, 8):
        other, z = (f + k // 4) % 2, (t + k) % 4
        gb_out.append(sems.remote(g1_s.at[2], g1_z.at[f * 4 + t], {"fsdp": other, "tp": z}, b0 + k, b0 + (k if k < 4 else 4 + (8 - k) % 4)))
    for cp in gb_out:
        cp.start()
    g1_z[f * 4 + t] = tot

    def put_wide(rows, v):
        ge[0, rows, :] = v[:, :256]
        ge[1, rows, :] = v[:, 256:]

    def put_narrow(rows, v):
        ge[2, rows, :] = v

    rz[0].s3(put_wide)
    lay_all.s3()
    for src, dst in ((ge.at[pl.ds(0, 2)], ge_o.at[pl.ds(0, 2)]), (lay, lay_o)):
        out_all.append(sems.local(src, dst))
        out_all[-1].start()
    for k in (0, 1):
        both(gat[k], "s5")
        out_all.append(sems.local(gall.at[k], gall_o.at[k]))
        out_all[-1].start()
    gt_all.s3()
    out_all.append(sems.local(gt, gt_o))
    out_all[-1].start()
    rz[1].s3(put_narrow)
    out_all.append(sems.local(ge.at[2], ge_o.at[2]))
    out_all[-1].start()
    for cp in gb_out:
        cp.wait_recv()
    tot = g1_z[0]
    for k in range(1, 8):
        tot = tot + g1_z[k]
    g1f[...] = jnp.where(f == 0, tot[0], tot[1])
    for cp in sg_out:
        cp.wait_recv()
    for src, dst in ((g1f, g1_o), (sg, sg_o)):
        out_all.append(sems.local(src, dst))
        out_all[-1].start()

    both((dx1, lay_all, gt_all, small_sum, gain_sum), "fin")
    for g in [rz] + [gat[k] for k in range(4)]:
        both(g, "fin")
    for cp in pz_out + sg_out + gb_out:
        cp.wait_send()
    for cp in out_all:
        cp.wait()


def finish_kernel(lay, gt, gall, sg, ge, g1, lo_o, gt_o, gq_o, go_o, gg_o, gk_o, gr_o, gi_o, gd_o, *s):
    (lay_v, gt_v, gall_v, sg_v, ge_v, g1_v, lo_w, gt_w, gall_w, gg_w, gk_w, gr_w, ge_w, sem) = s
    i = 0

    def copy(src, dst):
        nonlocal i
        cp = pltpu.make_async_copy(src, dst, sem.at[i])
        i += 1
        cp.start()
        return cp

    get = [copy(gall.at[k], gall_v.at[k]) for k in range(4)] + [copy(ge.at[k], ge_v.at[k]) for k in range(3)]
    get += [copy(gt, gt_v), copy(lay, lay_v), copy(sg, sg_v), copy(g1, g1_v)]
    put = []
    for k in range(4):
        get[k].wait()

        def body(j, _):
            rows = pl.ds(pl.multiple_of(j * 64, 64), 64)
            gall_w[k, rows, :] = gall_v[k, rows, :].astype(F32)
            return 0
        lax.fori_loop(0, 16, body, 0)
        put.append(copy(gall_w.at[k], gq_o.at[k] if k < 3 else go_o))
    for k in range(3):
        get[4 + k].wait()

        def body(j, _):
            rows = pl.ds(pl.multiple_of(j * 128, 128), 128)
            ge_w[k, rows, :] = ge_v[k, rows, :].astype(F32)
            return 0
        lax.fori_loop(0, 8, body, 0)
        put.append(copy(ge_w.at[k], gi_o.at[0, k] if k < 2 else gd_o.at[0]))
    get[7].wait()
    get[8].wait()
    for z in range(4):
        for m in range(2):
            gt_w[m, 16 * z:16 * z + 16, :] = gt_v[z, 16 * m:16 * m + 16, :].astype(F32)
            lo_w[m, 16 * z:16 * z + 16, :] = lay_v[z, 16 * m:16 * m + 16, :]
    put += [copy(gt_w, gt_o.at[:, 0]), copy(lo_w, lo_o.at[:, 0])]
    get[9].wait()
    for z in range(4):
        cols = slice(256 * z, 256 * z + 256)
        gr_w[:, cols] = sg_v[z, 0:16, :]
        gg_w[1:2, cols] = sg_v[z, 17:18, :]
    get[10].wait()
    for i8 in range(8):
        gg_w[0:1, 128 * i8:128 * i8 + 128] = g1_v[i8:i8 + 1, :]
    gk_w[...] = sg_v[0, 18:20, 0:64]
    put += [copy(gr_w, gr_o), copy(gg_w, gg_o), copy(gk_w, gk_o)]
    for cp in put:
        cp.wait()


def finish(lay, gt, gall, sg, ge, g1):
    sd = jax.ShapeDtypeStruct
    v = pltpu.VMEM
    return pl.pallas_call(
        finish_kernel,
        out_shape=[sd((2, 1, 64, 2048), BF), sd((2, 1, 64, 2048), F32), sd((3, 1024, 512), F32), sd((1024, 512), F32),
                   sd((2, 1024), F32), sd((2, 64), F32), sd((16, 1024), F32), sd((1, 2, 1024, 256), F32), sd((1, 1024, 256), F32)],
        in_specs=[ANY] * 6,
        out_specs=[ANY] * 9,
        scratch_shapes=[
            v((4, 32, 2048), BF), v((4, 32, 2048), BF), v((4, 1024, 512), BF), v((4, 32, 256), F32), v((3, 1024, 256), BF), v((8, 128), F32),
            v((2, 64, 2048), BF), v((2, 64, 2048), F32), v((4, 1024, 512), F32), v((2, 1024), F32), v((2, 64), F32), v((16, 1024), F32),
            v((3, 1024, 256), F32), pltpu.SemaphoreType.DMA((24,))],
        compiler_params=pltpu.CompilerParams(vmem_limit_bytes=62 << 20),
        name="finish",
    )(lay, gt, gall.reshape(4, 1024, 512), sg, ge, g1)


def back(tok, cot, fr):
    sd = jax.ShapeDtypeStruct
    v = pltpu.VMEM
    rings = []
    for _ in range(2):
        rings += Scatter2.scratch(16, 2048, 1024)
    for _ in range(8):
        rings += Scatter2.scratch(32, 512, 256)
    rings += ScatterZ.scratch(512) + ScatterZ.scratch(256)
    outs = pl.pallas_call(
        back_kernel,
        out_shape=[sd((4, 32, 2048), BF), sd((4, 32, 2048), BF), sd((4, 4, 4, 2, 32, 512), BF), sd((4, 32, 256), F32), sd((3, 1024, 256), BF), sd((8, 128), F32)],
        in_specs=[ANY] * 19,
        out_specs=[ANY] * 6,
        scratch_shapes=[
            v((4, 32, 256), F32), v((8, 128), F32),
            v((32, 2176), F32), v((4, 32, 2048), BF), v((4, 32, 2048), BF), v((3, 1024, 256), BF),
            v((2, 16, 2048), BF), v((2, 16, 2048), BF), v((2, 32, 16), F32), v((2, 32, 1024), F32), v((2, 128, 1024), BF), v((2, 128, 512), F32),
            v((2, 128, 512), BF), v((32, 2048), F32), v((3, 16, 64, HD), BF), v((512, HD), F32), v((512, 128), F32),
            v((2048, 1536), BF), v((2048, 512), BF), v((64, 256), F32), v((128, 256), F32), v((3, 1024, 1024), BF),
            v((4, 4, 2, 16, 2048), BF), v((2, 2, 4, 16, 1024), BF), v((2, 512, 512), BF), v((4, 32, 2048), BF),
            v((8, 64, HD), BF), v((8, 64, HD), BF), v((2, 512, HD), BF), v((2, 512, HD), BF), v((8, 64, HD), BF), v((8, 64, HD), BF), v((8, 2, 64, HD), BF), v((8, 2, 64, HD), BF),
            v((4, 4, 4, 2, 32, 512), BF),
            v((2, 128, 512), F32), v((2, 128, 1536), BF), v((4, 32, 2048), BF), v((2, 32, 1024), BF), v((2, 32, 2048), BF),
            v((2, 4, 32, 1024), BF), v((4, 4, 4, 2, 32, 512), BF), v((4, 2, 32, 512), BF),
            v((2, 32, 1024), F32), v((32, 1024), BF), v((32, 1024), BF), v((4, 32, 256), BF), v((3, 32, 256), BF),
            v((2, 32, 256), BF), v((2, 3, 32, 256), BF),
            v((3, 2, 8, 128), F32), v((2, 3, 2, 8, 128), F32), v((8, 2, 8, 128), F32),
            pltpu.SemaphoreType.DMA((304,)), pltpu.SemaphoreType.DMA((304,))] + rings,
        compiler_params=pltpu.CompilerParams(collective_id=1, has_side_effects=True, vmem_limit_bytes=62 << 20),
        name="back",
    )(fr["dxe"], tok, cot, fr["pr"], fr["sm"], fr["xc"], fr["p"], fr["oc"], fr["h1"], fr["qkv_r"], fr["of"], fr["e"], fr["rt"], jnp.asarray(rope_const()),
      fr["y"], fr["gw"], fr["yr"], fr["wq"], fr["wo"])
    return finish(*outs)


def local(tokens, routes, cotangent, qkv_weight, out_weight, norm_gains, qk_gains, router_weight, expert_in, expert_out):
    tok = tokens.reshape(2, 64, 2048)
    cot = cotangent.reshape(2, 64, 2048)
    small = (router_weight, norm_gains, qk_gains)
    routes = jnp.swapaxes(routes.reshape(2, 64, 8), 1, 2)
    fr = front(tok, cot, qkv_weight, out_weight, small, expert_in[0], expert_out[0], routes)
    return tuple(back(tok, cot, fr))


def solution(mesh):
    act = P(None, "fsdp", "ctx", None)
    weights = (P(None, "fsdp", "tp"), P("fsdp", "tp"), P(None, "fsdp"), P(None, "fsdp"), P(None, "fsdp"), P("ctx", None, "fsdp", "tp"), P("ctx", "fsdp", "tp"))
    return jax.shard_map(local, mesh=mesh, in_specs=(act, act, act) + weights, out_specs=(act, act) + weights, check_vma=False)
```
